32 devices in a mesh: dp: 4 (over y, core), expert: 8 (over z, x).
Axes of the slice: x: 2, y: 2, z: 4, core: 2. Of those that a mesh axis runs over, the one named last changes fastest.
Arguments:
- tokens: bfloat16 [4096, 1024], P(('dp', 'expert')), may hold values from -6 to 6
- routes: int32 [4096, 4], P(('dp', 'expert')), may hold values from 0 to 7, all different within a row; in each aligned block of 128 rows (0 to 127, 128 to 255, ...) at most 128 rows name the same one
- gates: float32 [4096, 4], P(('dp', 'expert')), may hold values from 0.05 to 0.5
- w_in: bfloat16 [8, 1024, 768], P('expert', 'dp'), may hold values from -6 to 6
- w_down: bfloat16 [8, 384, 1024], P('expert', 'dp'), may hold values from -6 to 6
- out_grad: bfloat16 [4096, 1024], P(('dp', 'expert')), may hold values from -6 to 6
Outputs:
- moe_out: bfloat16 [4096, 1024], P(('dp', 'expert'))
- token_grad: bfloat16 [4096, 1024], P(('dp', 'expert'))
- new_w_in: bfloat16 [8, 1024, 768], P('expert', 'dp')
- new_w_down: bfloat16 [8, 384, 1024], P('expert', 'dp')
The draws below stay inside these ranges and needn't reach their ends.
Inputs may be any that keep to these rules, and one draw needn't show every extreme that they name: `routes`: within one device's 128 tokens no expert is named more than 128 times, a bound that some block reaches; a token names 4 different experts.
All inputs are finite; a program needn't handle non-finite values.
Results may differ from the reference program's by a relative error of at most 0.014.
Values may be sent and summed in bfloat16 or wider, within the bound.
A program may use at most 64 MiB of HBM per device.

```python
import math
from functools import partial
import jax
import jax.numpy as jnp
import numpy as np
from jax import lax

D = 1024
F = 384
TOPK = 4
TOK_DEV = 128
EXPERTS = 8
CAP = 128
TOKENS = 4096
N_DP = 4
N_EXPERT = 8


def shard_levels(rng, shape, split, smallest, largest):
    def one(dim, shards_of):
        draws = jax.random.uniform(jax.random.fold_in(jax.random.fold_in(rng, 6), dim), (shards_of,), jnp.float32, smallest / len(split), largest / len(split))
        return jnp.repeat(jnp.exp(draws), shape[dim] // shards_of).reshape((-1,) + (1,) * (len(shape) - dim - 1))

    loudness = one(*split[0])
    for cut in split[1:]:
        loudness = loudness * one(*cut)
    return loudness


def deal_out(rng, own, number, rows, count, top, bound, skew):
    ranking = jax.random.permutation(rng, count)
    crowded, ordinary = load_shares(count, rows * top, bound, skew, True), load_shares(count, rows * top, bound, skew, False)
    places = jnp.arange(count)

    def named(lengths, turn):
        used = int((lengths > 0).sum())
        fixed = max(1, used // 4)
        shifted = fixed + (places - fixed + turn * (used - fixed)) % max(1, count - fixed)
        return jnp.zeros((count,), jnp.int32).at[ranking[jnp.where(places < fixed, places, shifted)]].set(jnp.asarray(lengths, jnp.int32))

    lengths = jnp.where(number % 4 == 0, named(crowded, number // 4), named(ordinary, number - number // 4 - 1))
    mixed = jax.random.permutation(jax.random.fold_in(own, 3), count)
    giver, sink = mixed[0:count // 2 * 2:2], mixed[1:count // 2 * 2:2]
    margin = jnp.minimum(lengths[giver] - 1, bound - lengths[sink]) // 2
    margin = jnp.where((giver == ranking[0]) | (sink == ranking[0]) | (lengths[sink] == 0), 0, jnp.maximum(margin, 0))
    shifted = jax.random.randint(jax.random.fold_in(own, 4), (count // 2,), 0, 1 << 20) % (margin + 1)
    lengths = lengths.at[giver].add(-shifted).at[sink].add(shifted)
    items = jnp.searchsorted(jnp.cumsum(lengths), jnp.arange(rows * top), side="right").astype(jnp.int32)
    listing = items.reshape(top, rows).T
    listing = listing[jax.random.permutation(jax.random.fold_in(own, 1), rows)]
    turn = jax.random.randint(jax.random.fold_in(own, 2), (rows, 1), 0, top)
    return jnp.take_along_axis(listing, (jnp.arange(top)[None, :] + turn) % top, axis=1)


def load_shares(amount, total, most, slope, full):
    weights = [(1 << 20) // math.isqrt(rank ** slope) + 1 for rank in range(1, amount + 1)]
    largest = most if full else min(most, max(-(-total // amount), total * weights[0] // sum(weights)))
    least = 1 if total - largest >= amount - 1 else 0
    holding, spare = [largest] + [least] * (amount - 1), total - largest - least * (amount - 1)
    while spare > 0:
        free = [i for i in range(1, amount) if holding[i] < largest] or [i for i in range(1, amount) if holding[i] < most]
        mass, left = sum([weights[i] for i in free]), spare
        for i in free:
            extra = min(most - holding[i], max(1, left * weights[i] // mass), spare)
            holding[i] = holding[i] + extra
            spare = spare - extra
    return np.array(holding)


def centred(rng, shape, spread, limit, cuts=(), kind=jnp.bfloat16):
    values = jax.random.normal(rng, shape, jnp.float32) * spread
    if len(cuts) > 0:
        values = shard_levels(rng, shape, cuts, -0.22, 0.18) * values
    return jnp.clip(values, min=-limit, max=limit).astype(kind)


def setup_inputs(seed: int = 0) -> dict:
    keys = jax.random.split(jax.random.key(seed), 7)
    tokens = centred(keys[0], (TOKENS, D), 1.0, 6.0, ((0, 32),))
    routes_keys = jax.random.split(jax.random.fold_in(keys[1], 1), TOKENS // TOK_DEV)
    routes_turns = jax.random.permutation(jax.random.fold_in(keys[1], 3), TOKENS // TOK_DEV)
    routes = jax.vmap(lambda own, number: deal_out(jax.random.fold_in(keys[1], 2), own, number, TOK_DEV, EXPERTS, TOPK, CAP, 2))(routes_keys, routes_turns).reshape((TOKENS, TOPK))
    gates = jnp.clip(jnp.exp(math.log(0.5) - 2.3025851 * jax.random.uniform(keys[2], (TOKENS, TOPK), jnp.float32) ** shard_levels(keys[2], (TOKENS, TOPK), ((0, 32),), -0.2, 0.2)), 0.05, 0.5)
    w_in = centred(keys[3], (EXPERTS, D, 2 * F), 1.0, 6.0, ((0, 8), (1, 4)))
    w_down = centred(keys[4], (EXPERTS, F, D), 1.0, 6.0, ((0, 8), (1, 4)))
    out_grad = centred(keys[5], (TOKENS, D), 1.0, 6.0, ((0, 32),))
    return {"tokens": tokens, "routes": routes, "gates": gates, "w_in": w_in, "w_down": w_down, "out_grad": out_grad}


step_rate = 0.5


def slot_numbers(route_rows, experts, capacity):
    flat_routes = route_rows.reshape(-1)
    one_hot = (flat_routes[:, None] == jnp.arange(experts, dtype=jnp.int32)[None, :]).astype(jnp.int32)
    running = jnp.cumsum(one_hot, axis=0)
    position = jnp.sum(one_hot * running, axis=1) - 1
    return (flat_routes * capacity + position).astype(jnp.int32)


def place_rows(rows, slot_index, total):
    return jnp.zeros((total, rows.shape[-1]), rows.dtype).at[slot_index].set(rows)


def pick_rows(rows, slot_index):
    return rows[slot_index]


def reference(tokens, routes, gates, w_in, w_down, out_grad):
    experts = EXPERTS
    capacity = CAP
    rows_in = TOK_DEV * TOPK
    token_of = jnp.arange(rows_in, dtype=jnp.int32) // TOPK
    scale_in = D ** -0.5
    scale_down = F ** -0.5
    total = experts * capacity

    def to_experts(sent):
        return sent.reshape(N_EXPERT, experts, capacity, D).transpose(1, 0, 2, 3).reshape(experts, N_EXPERT * capacity, D)

    def to_sources(done):
        return done.reshape(experts, N_EXPERT, capacity, D).transpose(1, 0, 2, 3).reshape(N_EXPERT, total, D)

    def group_step(totals, group_items):
        tok_group, route_group, gate_group, grad_group = group_items
        slot_index = jax.vmap(partial(slot_numbers, experts=experts, capacity=capacity))(route_group)
        placer = jax.vmap(partial(place_rows, total=total))
        send_inputs = placer(tok_group[:, token_of], slot_index)
        scaled = (gate_group.reshape(N_EXPERT, rows_in, 1) * grad_group[:, token_of].astype(jnp.float32)).astype(jnp.bfloat16)
        send_grads = placer(scaled, slot_index)
        inputs = to_experts(send_inputs)
        grad_rows = to_experts(send_grads)
        projected = jnp.einsum("erd,edj->erj", inputs.astype(jnp.float32), w_in.astype(jnp.float32)) * scale_in
        gate_part = projected[..., :F]
        up_part = projected[..., F:]
        activation = (jax.nn.silu(gate_part) * up_part).astype(jnp.bfloat16)
        results = (jnp.einsum("erf,efd->erd", activation.astype(jnp.float32), w_down.astype(jnp.float32)) * scale_down).astype(jnp.bfloat16)
        grad_act = jnp.einsum("erd,efd->erf", grad_rows.astype(jnp.float32), w_down.astype(jnp.float32)) * scale_down
        sigmoid_gate = jax.nn.sigmoid(gate_part)
        grad_gate = grad_act * up_part * sigmoid_gate * (1.0 + gate_part * (1.0 - sigmoid_gate))
        grad_up = grad_act * jax.nn.silu(gate_part)
        grad_hidden = jnp.concatenate([grad_gate, grad_up], axis=-1).astype(jnp.bfloat16)
        grad_inputs = (jnp.einsum("erj,edj->erd", grad_hidden.astype(jnp.float32), w_in.astype(jnp.float32)) * scale_in).astype(jnp.bfloat16)
        grad_in = (jnp.einsum("erd,erj->edj", inputs.astype(jnp.float32), grad_hidden.astype(jnp.float32)) * scale_in).astype(jnp.bfloat16)
        grad_down = (jnp.einsum("erf,erd->efd", activation.astype(jnp.float32), grad_rows.astype(jnp.float32)) * scale_down).astype(jnp.bfloat16)
        picked = jax.vmap(pick_rows)(to_sources(results), slot_index).astype(jnp.float32)
        picked = picked.reshape(N_EXPERT, TOK_DEV, TOPK, D)
        moe_group = jnp.sum(picked * gate_group[..., None], axis=2).astype(jnp.bfloat16)
        back_rows = jax.vmap(pick_rows)(to_sources(grad_inputs), slot_index).astype(jnp.float32)
        token_group = jnp.sum(back_rows.reshape(N_EXPERT, TOK_DEV, TOPK, D), axis=2).astype(jnp.bfloat16)
        new_totals = (totals[0] + grad_in.astype(jnp.float32), totals[1] + grad_down.astype(jnp.float32))
        return new_totals, (moe_group, token_group)

    group_items = (tokens.reshape(N_DP, N_EXPERT, TOK_DEV, D),
                   routes.reshape(N_DP, N_EXPERT, TOK_DEV, TOPK),
                   gates.reshape(N_DP, N_EXPERT, TOK_DEV, TOPK),
                   out_grad.reshape(N_DP, N_EXPERT, TOK_DEV, D))
    start_totals = (jnp.zeros(w_in.shape, jnp.float32), jnp.zeros(w_down.shape, jnp.float32))
    totals, outputs = lax.scan(group_step, start_totals, group_items)
    moe_out = outputs[0].reshape(TOKENS, D)
    token_grad = outputs[1].reshape(TOKENS, D)
    new_w_in = (w_in.astype(jnp.float32) - step_rate * totals[0]).astype(jnp.bfloat16)
    new_w_down = (w_down.astype(jnp.float32) - step_rate * totals[1]).astype(jnp.bfloat16)
    return (moe_out, token_grad, new_w_in, new_w_down)
```

```python
import jax
import jax.numpy as jnp
from jax import lax
from jax.sharding import PartitionSpec as P

step_rate = 0.5


def expert_gates(routes, gates, experts):
    hit = routes[:, :, None] == jnp.arange(experts, dtype=jnp.int32)[None, None, :]
    return jnp.sum(jnp.where(hit, gates[:, :, None], 0.0), axis=1)


def body(tokens, routes, gates, w_in, w_down, out_grad):
    model_width = tokens.shape[1]
    hidden = w_in.shape[2] // 2
    per_device = w_in.shape[0]
    experts = per_device * lax.axis_size("expert")
    scale_in = model_width**-0.5
    scale_down = hidden**-0.5
    f32 = jnp.float32
    full_in = lax.all_gather(w_in, "dp", axis=1, tiled=True)
    all_tokens = lax.all_gather(tokens, "expert", axis=0, tiled=True)
    all_grads = lax.all_gather(out_grad, "expert", axis=0, tiled=True)
    full_down = lax.all_gather(w_down, "dp", axis=1, tiled=True)
    weight = lax.all_gather(expert_gates(routes, gates, experts), "expert", axis=0, tiled=True)
    first = lax.axis_index("expert") * per_device
    moe, back, grads_in, grads_down = 0.0, 0.0, [], []
    for local in range(per_device):
        win, wdown = full_in[local], full_down[local]
        g = lax.dynamic_slice_in_dim(weight, first + local, 1, axis=1)
        proj = jnp.dot(all_tokens, win, preferred_element_type=f32) * scale_in
        gate, up = proj[:, :hidden], proj[:, hidden:]
        sig = jax.nn.sigmoid(gate)
        act = (gate * sig * up).astype(jnp.bfloat16)
        y = (jnp.dot(act, wdown, preferred_element_type=f32) * scale_down).astype(jnp.bfloat16)
        moe = moe + g * y.astype(f32)
        dy = (g * all_grads.astype(f32)).astype(jnp.bfloat16)
        dact = lax.dot_general(dy, wdown, (((1,), (1,)), ((), ())), preferred_element_type=f32) * scale_down
        dproj = jnp.concatenate(
            [dact * up * sig * (1.0 + gate * (1.0 - sig)), dact * gate * sig], axis=-1
        ).astype(jnp.bfloat16)
        dx = lax.dot_general(dproj, win, (((1,), (1,)), ((), ())), preferred_element_type=f32) * scale_in
        back = back + dx.astype(jnp.bfloat16).astype(f32)
        grads_in.append(
            (lax.dot_general(all_tokens, dproj, (((0,), (0,)), ((), ())), preferred_element_type=f32) * scale_in).astype(jnp.bfloat16)
        )
        grads_down.append(
            (lax.dot_general(act, dy, (((0,), (0,)), ((), ())), preferred_element_type=f32) * scale_down).astype(jnp.bfloat16)
        )
    moe_out = lax.psum_scatter(moe.astype(jnp.bfloat16), "expert", scatter_dimension=0, tiled=True)
    token_grad = lax.psum_scatter(back.astype(jnp.bfloat16), "expert", scatter_dimension=0, tiled=True)
    sum_in = lax.psum_scatter(jnp.stack(grads_in), "dp", scatter_dimension=1, tiled=True)
    sum_down = lax.psum_scatter(jnp.stack(grads_down), "dp", scatter_dimension=1, tiled=True)
    new_w_in = (w_in.astype(f32) - step_rate * sum_in.astype(f32)).astype(jnp.bfloat16)
    new_w_down = (w_down.astype(f32) - step_rate * sum_down.astype(f32)).astype(jnp.bfloat16)
    return (moe_out, token_grad, new_w_in, new_w_down)


def solution(mesh):
    return jax.shard_map(
        body,
        mesh=mesh,
        in_specs=(
            P(("dp", "expert"), None),
            P(("dp", "expert"), None),
            P(("dp", "expert"), None),
            P("expert", "dp", None),
            P("expert", "dp", None),
            P(("dp", "expert"), None),
        ),
        out_specs=(
            P(("dp", "expert"), None),
            P(("dp", "expert"), None),
            P("expert", "dp", None),
            P("expert", "dp", None),
        ),
        check_vma=False,
    )
```

```python
import jax
import jax.numpy as jnp
from jax import lax
from jax.experimental import pallas as pl
from jax.experimental.pallas import tpu as pltpu
from jax.sharding import PartitionSpec as P

step_rate = 0.5


def expert_gates(routes, gates, experts):
    hit = routes[:, :, None] == jnp.arange(experts, dtype=jnp.int32)[None, None, :]
    return jnp.sum(jnp.where(hit, gates[:, :, None], 0.0), axis=1)


def body(tokens, routes, gates, w_in, w_down, out_grad):
    model_width = tokens.shape[1]
    hidden = w_in.shape[2] // 2
    per_device = w_in.shape[0]
    experts = per_device * lax.axis_size("expert")
    scale_in = model_width**-0.5
    scale_down = hidden**-0.5
    f32 = jnp.float32
    full_in = lax.all_gather(w_in, "dp", axis=1, tiled=True)
    all_tokens = lax.all_gather(tokens, "expert", axis=0, tiled=True)
    all_grads = lax.all_gather(out_grad, "expert", axis=0, tiled=True)
    full_down = lax.all_gather(w_down, "dp", axis=1, tiled=True)
    weight = lax.all_gather(expert_gates(routes, gates, experts), "expert", axis=0, tiled=True)
    first = lax.axis_index("expert") * per_device
    moe, back, grads_in, grads_down = 0.0, 0.0, [], []
    for local in range(per_device):
        win, wdown = full_in[local], full_down[local]
        g = lax.dynamic_slice_in_dim(weight, first + local, 1, axis=1)
        proj = jnp.dot(all_tokens, win, preferred_element_type=f32) * scale_in
        gate, up = proj[:, :hidden], proj[:, hidden:]
        sig = jax.nn.sigmoid(gate)
        act = (gate * sig * up).astype(jnp.bfloat16)
        y = (jnp.dot(act, wdown, preferred_element_type=f32) * scale_down).astype(jnp.bfloat16)
        moe = moe + g * y.astype(f32)
        dy = (g * all_grads.astype(f32)).astype(jnp.bfloat16)
        dact = lax.dot_general(dy, wdown, (((1,), (1,)), ((), ())), preferred_element_type=f32) * scale_down
        dproj = jnp.concatenate(
            [dact * up * sig * (1.0 + gate * (1.0 - sig)), dact * gate * sig], axis=-1
        ).astype(jnp.bfloat16)
        dx = lax.dot_general(dproj, win, (((1,), (1,)), ((), ())), preferred_element_type=f32) * scale_in
        back = back + dx.astype(jnp.bfloat16).astype(f32)
        grads_in.append(
            (lax.dot_general(all_tokens, dproj, (((0,), (0,)), ((), ())), preferred_element_type=f32) * scale_in).astype(jnp.bfloat16)
        )
        grads_down.append(
            (lax.dot_general(act, dy, (((0,), (0,)), ((), ())), preferred_element_type=f32) * scale_down).astype(jnp.bfloat16)
        )
    moe_out = lax.psum_scatter(moe.astype(jnp.bfloat16), "expert", scatter_dimension=0, tiled=True)
    token_grad = lax.psum_scatter(back.astype(jnp.bfloat16), "expert", scatter_dimension=0, tiled=True)
    sum_in = lax.psum_scatter(jnp.stack(grads_in), "dp", scatter_dimension=1, tiled=True)
    sum_down = lax.psum_scatter(jnp.stack(grads_down), "dp", scatter_dimension=1, tiled=True)
    new_w_in = (w_in.astype(f32) - step_rate * sum_in.astype(f32)).astype(jnp.bfloat16)
    new_w_down = (w_down.astype(f32) - step_rate * sum_down.astype(f32)).astype(jnp.bfloat16)
    return (moe_out, token_grad, new_w_in, new_w_down)


MESH = pl.DeviceIdType.MESH
f32 = jnp.float32
bf16 = jnp.bfloat16


def xor4(z, j):
    a, b, c, d = z // 2, z % 2, j // 2, j % 2
    return 2 * (a + c - 2 * a * c) + b + d - 2 * b * d


def fused_kernel(
    tok_ref, grad_ref, g_ref, win_ref, wdown_ref,
    moe_ref, back_ref, nwin_ref, nwdown_ref,
    rows_all, g_all, win, wdown, dproj_all, act_all, dy_all, part, rx, rz,
    gin, gdown, gin_core, gdown_core, gin_y, gdown_y,
    g_send, g_recv, w_send, w_recv, z_send, x_send, row_recv,
    rx_send, rx_recv, rz_send, rz_recv, gc_send, gc_recv, gy_send, gy_recv,
):
    dp = lax.axis_index("dp")
    me = lax.axis_index("expert")
    y, core = dp // 2, dp % 2
    z, x = me // 2, me % 2
    n = tok_ref.shape[0]
    hidden = wdown.shape[0]
    scale_in = win.shape[0] ** -0.5
    scale_down = hidden**-0.5
    q_in, q_down = win_ref.shape[0], wdown_ref.shape[0]
    core_peer = (2 * y + 1 - core, me)
    y_peer = (2 * (1 - y) + core, me)
    x_peer = (dp, 2 * z + 1 - x)
    inner = (z + 1) // 2 % 2

    def copy(src, dst, ssem, rsem, device):
        return pltpu.make_async_remote_copy(
            src_ref=src, dst_ref=dst, send_sem=ssem, recv_sem=rsem,
            device_id=device, device_id_type=MESH,
        )

    def rows(s, size):
        return pl.ds(pl.multiple_of(s * size, 16), size)

    def order(j):
        far = j // 2
        swapped = xor4(z, j + inner * far * (5 - 2 * j))
        return swapped

    rows_all[0, rows(me, n), :] = tok_ref[...]
    rows_all[1, rows(me, n), :] = grad_ref[...]
    g_all[me] = g_ref[...]
    win[rows(dp, q_in), :] = win_ref[...]
    wdown[rows(dp, q_down), :] = wdown_ref[...]

    barrier = pltpu.get_barrier_semaphore()
    for k in range(1, 8):
        pl.semaphore_signal(barrier, inc=1, device_id=(dp, (me + k) % 8), device_id_type=MESH)
    pl.semaphore_signal(barrier, inc=1, device_id=core_peer, device_id_type=MESH)
    pl.semaphore_signal(barrier, inc=1, device_id=y_peer, device_id_type=MESH)
    pl.semaphore_wait(barrier, 9)

    def w_copy(w, k):
        ref, size = ((win, q_in), (wdown, q_down))[w]
        source = 2 * (1 - y) + core if k == 2 else dp
        block = ref.at[rows(source, size), :]
        return copy(block, block, w_send.at[w, k], w_recv.at[w, source], y_peer if k == 0 else core_peer)

    def w_arrive(w, source):
        ref, size = ((win, q_in), (wdown, q_down))[w]
        block = ref.at[rows(source, size), :]
        copy(block, block, w_send.at[w, 0], w_recv.at[w, source], y_peer).wait_recv()

    def g_copy(k):
        return copy(g_all.at[me], g_all.at[me], g_send.at[k - 1], g_recv.at[me], (dp, (me + k) % 8))

    def z_copy(a, j, up):
        s = order(j)
        block = rows_all.at[a, rows(2 * s + x, n), :]
        target = me + 2 if up else me - 2
        return copy(block, block, z_send.at[a, j, up], row_recv.at[a, 2 * s + x], (dp, target))

    def x_copy(a, j):
        s = order(j)
        block = rows_all.at[a, rows(2 * s + x, n), :]
        return copy(block, block, x_send.at[a, j], row_recv.at[a, 2 * s + x], x_peer)

    def row_arrive(a, slot):
        block = rows_all.at[a, rows(slot, n), :]
        copy(block, block, x_send.at[a, 0], row_recv.at[a, slot], x_peer).wait_recv()

    def z_conditions(j):
        s = order(j)
        return (z < 3) & (s <= z), (z > 0) & (s >= z)

    def forward(j):
        go_up, go_down = z_conditions(j)
        for a in range(2):
            if j > 0:
                row_arrive(a, 2 * order(j) + x)

            @pl.when(go_up)
            def _():
                z_copy(a, j, 1).start()

            @pl.when(go_down)
            def _():
                z_copy(a, j, 0).start()

            x_copy(a, j).start()

    for w in range(2):
        w_copy(w, 0).start()
        w_copy(w, 1).start()
    for k in range(1, 8):
        g_copy(k).start()
    forward(0)
    forward(1)
    for w in range(2):
        w_arrive(w, 2 * (1 - y) + core)
        w_copy(w, 2).start()
    forward(2)
    for k in range(1, 8):
        s = (me + k) % 8
        copy(g_all.at[s], g_all.at[s], g_send.at[0], g_recv.at[s], x_peer).wait_recv()
    for w in range(2):
        w_arrive(w, 2 * y + 1 - core)
        w_arrive(w, 2 * (1 - y) + 1 - core)

    nt = (((1,), (1,)), ((), ()))
    tn = (((0,), (0,)), ((), ()))

    def compute(slot):
        at = rows(slot, n)
        by_expert = jnp.transpose(g_all[slot], (1, 0))
        lane = lax.broadcasted_iota(jnp.int32, by_expert.shape, 1)
        g = jnp.sum(jnp.where(lane == me, by_expert, 0.0), axis=1, keepdims=True)
        dy = (g * rows_all[1, at, :].astype(f32)).astype(bf16)
        dy_all[at, :] = dy
        proj = jnp.dot(rows_all[0, at, :], win[...], preferred_element_type=f32) * scale_in
        dact = lax.dot_general(dy, wdown[...], nt, preferred_element_type=f32) * scale_down
        gate, up = proj[:, :hidden], proj[:, hidden:]
        sig = jax.nn.sigmoid(gate)
        silu = gate * sig
        act = (silu * up).astype(bf16)
        act_all[at, :] = act
        dproj_all[at, :hidden] = (dact * up * sig * (1.0 + gate * (1.0 - sig))).astype(bf16)
        dproj_all[at, hidden:] = (dact * silu).astype(bf16)
        out = (jnp.dot(act, wdown[...], preferred_element_type=f32) * scale_down).astype(bf16)
        part[0, at, :] = (g * out.astype(f32)).astype(bf16)
        dx = lax.dot_general(dproj_all[at, :], win[...], nt, preferred_element_type=f32) * scale_in
        part[1, at, :] = dx.astype(bf16)

    def rx_copy(a, s):
        block = part.at[a, rows(2 * s + 1 - x, n), :]
        return copy(block, rx.at[a, s], rx_send.at[a, s], rx_recv.at[a, s], x_peer)

    def step(j, carry):
        @pl.when(j == 1)
        def _():
            forward(3)

        s = order(j)
        compute(2 * s + x)
        row_arrive(0, 2 * s + 1 - x)
        row_arrive(1, 2 * s + 1 - x)
        compute(2 * s + 1 - x)
        rx_copy(0, s).start()
        rx_copy(1, s).start()
        return carry

    lax.fori_loop(0, 4, step, 0)

    for q in range(4):
        gin[q * q_in:(q + 1) * q_in, :] = (
            lax.dot_general(rows_all[0, :, q * q_in:(q + 1) * q_in], dproj_all[...], tn, preferred_element_type=f32) * scale_in
        ).astype(bf16)
    gdown[...] = (lax.dot_general(act_all[...], dy_all[...], tn, preferred_element_type=f32) * scale_down).astype(bf16)

    def gc_copy(w, yy):
        ref, size, dst = ((gin, q_in, gin_core), (gdown, q_down, gdown_core))[w]
        return copy(ref.at[rows(2 * yy + 1 - core, size), :], dst.at[yy], gc_send.at[w, yy], gc_recv.at[w, yy], core_peer)

    def gy_copy(w):
        ref, size, dst = ((gin, q_in, gin_y), (gdown, q_down, gdown_y))[w]
        return copy(ref.at[rows(2 * (1 - y) + core, size), :], dst, gy_send.at[w], gy_recv.at[w], y_peer)

    for w in range(2):
        for yy in range(2):
            gc_copy(w, yy).start()

    def line_copy(a, t, up):
        if up:
            slot, target = t, me + 2
        else:
            slot, target = t + (4 - t) * (1 - jnp.minimum(z - 1 - t, 1)), me - 2
        return copy(part.at[a, rows(2 * t + x, n), :], rz.at[a, slot], rz_send.at[a, t], rz_recv.at[a, slot], (dp, target))

    def line_arrive(a, slot):
        copy(rz.at[a, slot], rz.at[a, slot], rz_send.at[a, 0], rz_recv.at[a, slot], x_peer).wait_recv()

    def line(t):
        for a in range(2):
            at = rows(2 * t + x, n)

            @pl.when(z != t)
            def _():
                rx_copy(a, t).wait_recv()

                @pl.when(((z < t) & (z > 0)) | ((z > t) & (z < 3)))
                def _():
                    line_arrive(a, t)
                    part[a, at, :] = (
                        part[a, at, :].astype(f32) + rx[a, t].astype(f32) + rz[a, t].astype(f32)
                    ).astype(bf16)

                @pl.when(((z < t) & (z == 0)) | ((z > t) & (z == 3)))
                def _():
                    part[a, at, :] = (part[a, at, :].astype(f32) + rx[a, t].astype(f32)).astype(bf16)

            @pl.when(z < t)
            def _():
                line_copy(a, t, 1).start()

            @pl.when(z > t)
            def _():
                line_copy(a, t, 0).start()

    line(1)
    line(2)
    for w in range(2):
        ref, size, got = ((gin, q_in, gin_core), (gdown, q_down, gdown_core))[w]
        gc_copy(w, 0).wait_recv()
        gc_copy(w, 1).wait_recv()
        at = rows(2 * (1 - y) + core, size)
        ref[at, :] = (ref[at, :].astype(f32) + got[1 - y].astype(f32)).astype(bf16)
        gy_copy(w).start()
    line(0)
    line(3)

    for w in range(2):
        ref, size, got, far, old, new = (
            (gin, q_in, gin_core, gin_y, win_ref, nwin_ref),
            (gdown, q_down, gdown_core, gdown_y, wdown_ref, nwdown_ref),
        )[w]
        gy_copy(w).wait_recv()
        total = ref[rows(dp, size), :].astype(f32) + got[y].astype(f32) + far[...].astype(f32)
        new[...] = (old[...].astype(f32) - step_rate * total).astype(bf16)

    for a in range(2):
        out = (moe_ref, back_ref)[a]
        rx_copy(a, z).wait_recv()
        own = part[a, rows(me, n), :].astype(f32) + rx[a, z].astype(f32)

        @pl.when(z == 0)
        def _():
            line_arrive(a, 4)
            out[...] = (own + rz[a, 4].astype(f32)).astype(bf16)

        @pl.when(z == 3)
        def _():
            line_arrive(a, 3)
            out[...] = (own + rz[a, 3].astype(f32)).astype(bf16)

        @pl.when((z > 0) & (z < 3))
        def _():
            line_arrive(a, z)
            line_arrive(a, 4)
            out[...] = (own + rz[a, z].astype(f32) + rz[a, 4].astype(f32)).astype(bf16)

    for w in range(2):
        for k in range(3):
            w_copy(w, k).wait_send()
        for yy in range(2):
            gc_copy(w, yy).wait_send()
        gy_copy(w).wait_send()
    for k in range(1, 8):
        g_copy(k).wait_send()
    for a in range(2):
        for j in range(4):
            go_up, go_down = z_conditions(j)

            @pl.when(go_up)
            def _():
                z_copy(a, j, 1).wait_send()

            @pl.when(go_down)
            def _():
                z_copy(a, j, 0).wait_send()

            x_copy(a, j).wait_send()
            rx_copy(a, j).wait_send()

            @pl.when(z < j)
            def _():
                line_copy(a, j, 1).wait_send()

            @pl.when(z > j)
            def _():
                line_copy(a, j, 0).wait_send()


def fused_body(tokens, routes, gates, w_in, w_down, out_grad):
    n, width = tokens.shape
    hidden = w_in.shape[2] // 2
    q_in, q_down = w_in.shape[1], w_down.shape[1]
    hit = routes.T[:, None, :] == jnp.arange(8, dtype=jnp.int32)[None, :, None]
    weight = jnp.sum(jnp.where(hit, gates.T[:, None, :], 0.0), axis=0)
    vmem = pl.BlockSpec(memory_space=pltpu.VMEM)
    dma = pltpu.SemaphoreType.DMA
    buf = pltpu.VMEM
    outs = pl.pallas_call(
        fused_kernel,
        out_shape=(
            jax.ShapeDtypeStruct((n, width), bf16),
            jax.ShapeDtypeStruct((n, width), bf16),
            jax.ShapeDtypeStruct((q_in, 2 * hidden), bf16),
            jax.ShapeDtypeStruct((q_down, width), bf16),
        ),
        in_specs=[vmem] * 5,
        out_specs=(vmem,) * 4,
        scratch_shapes=[
            buf((2, 8 * n, width), bf16),
            buf((8, 8, n), f32),
            buf((4 * q_in, 2 * hidden), bf16),
            buf((4 * q_down, width), bf16),
            buf((8 * n, 2 * hidden), bf16),
            buf((8 * n, hidden), bf16),
            buf((8 * n, width), bf16),
            buf((2, 8 * n, width), bf16),
            buf((2, 4, n, width), bf16),
            buf((2, 5, n, width), bf16),
            buf((4 * q_in, 2 * hidden), bf16),
            buf((4 * q_down, width), bf16),
            buf((2, q_in, 2 * hidden), bf16),
            buf((2, q_down, width), bf16),
            buf((q_in, 2 * hidden), bf16),
            buf((q_down, width), bf16),
            dma((7,)), dma((8,)), dma((2, 3)), dma((2, 4)), dma((2, 4, 2)), dma((2, 4)), dma((2, 8)),
            dma((2, 4)), dma((2, 4)), dma((2, 4)), dma((2, 5)), dma((2, 2)), dma((2, 2)), dma((2,)), dma((2,)),
        ],
        compiler_params=pltpu.CompilerParams(
            collective_id=0, has_side_effects=True, vmem_limit_bytes=48 * 1024 * 1024
        ),
    )(tokens, out_grad, weight, w_in[0], w_down[0])
    return (outs[0], outs[1], outs[2][None], outs[3][None])


def solution(mesh):
    fused = mesh.shape["dp"] == 4 and mesh.shape["expert"] == 8
    return jax.shard_map(
        fused_body if fused else body,
        mesh=mesh,
        in_specs=(
            P(("dp", "expert"), None),
            P(("dp", "expert"), None),
            P(("dp", "expert"), None),
            P("expert", "dp", None),
            P("expert", "dp", None),
            P(("dp", "expert"), None),
        ),
        out_specs=(
            P(("dp", "expert"), None),
            P(("dp", "expert"), None),
            P("expert", "dp", None),
            P("expert", "dp", None),
        ),
        check_vma=False,
    )
```

```python
import jax
import jax.numpy as jnp
from jax import lax
from jax.experimental import pallas as pl
from jax.experimental.pallas import tpu as pltpu
from jax.sharding import PartitionSpec as P

step_rate = 0.5


def expert_gates(routes, gates, experts):
    hit = routes[:, :, None] == jnp.arange(experts, dtype=jnp.int32)[None, None, :]
    return jnp.sum(jnp.where(hit, gates[:, :, None], 0.0), axis=1)


def body(tokens, routes, gates, w_in, w_down, out_grad):
    model_width = tokens.shape[1]
    hidden = w_in.shape[2] // 2
    per_device = w_in.shape[0]
    experts = per_device * lax.axis_size("expert")
    scale_in = model_width**-0.5
    scale_down = hidden**-0.5
    f32 = jnp.float32
    full_in = lax.all_gather(w_in, "dp", axis=1, tiled=True)
    all_tokens = lax.all_gather(tokens, "expert", axis=0, tiled=True)
    all_grads = lax.all_gather(out_grad, "expert", axis=0, tiled=True)
    full_down = lax.all_gather(w_down, "dp", axis=1, tiled=True)
    weight = lax.all_gather(expert_gates(routes, gates, experts), "expert", axis=0, tiled=True)
    first = lax.axis_index("expert") * per_device
    moe, back, grads_in, grads_down = 0.0, 0.0, [], []
    for local in range(per_device):
        win, wdown = full_in[local], full_down[local]
        g = lax.dynamic_slice_in_dim(weight, first + local, 1, axis=1)
        proj = jnp.dot(all_tokens, win, preferred_element_type=f32) * scale_in
        gate, up = proj[:, :hidden], proj[:, hidden:]
        sig = jax.nn.sigmoid(gate)
        act = (gate * sig * up).astype(jnp.bfloat16)
        y = (jnp.dot(act, wdown, preferred_element_type=f32) * scale_down).astype(jnp.bfloat16)
        moe = moe + g * y.astype(f32)
        dy = (g * all_grads.astype(f32)).astype(jnp.bfloat16)
        dact = lax.dot_general(dy, wdown, (((1,), (1,)), ((), ())), preferred_element_type=f32) * scale_down
        dproj = jnp.concatenate(
            [dact * up * sig * (1.0 + gate * (1.0 - sig)), dact * gate * sig], axis=-1
        ).astype(jnp.bfloat16)
        dx = lax.dot_general(dproj, win, (((1,), (1,)), ((), ())), preferred_element_type=f32) * scale_in
        back = back + dx.astype(jnp.bfloat16).astype(f32)
        grads_in.append(
            (lax.dot_general(all_tokens, dproj, (((0,), (0,)), ((), ())), preferred_element_type=f32) * scale_in).astype(jnp.bfloat16)
        )
        grads_down.append(
            (lax.dot_general(act, dy, (((0,), (0,)), ((), ())), preferred_element_type=f32) * scale_down).astype(jnp.bfloat16)
        )
    moe_out = lax.psum_scatter(moe.astype(jnp.bfloat16), "expert", scatter_dimension=0, tiled=True)
    token_grad = lax.psum_scatter(back.astype(jnp.bfloat16), "expert", scatter_dimension=0, tiled=True)
    sum_in = lax.psum_scatter(jnp.stack(grads_in), "dp", scatter_dimension=1, tiled=True)
    sum_down = lax.psum_scatter(jnp.stack(grads_down), "dp", scatter_dimension=1, tiled=True)
    new_w_in = (w_in.astype(f32) - step_rate * sum_in.astype(f32)).astype(jnp.bfloat16)
    new_w_down = (w_down.astype(f32) - step_rate * sum_down.astype(f32)).astype(jnp.bfloat16)
    return (moe_out, token_grad, new_w_in, new_w_down)


MESH = pl.DeviceIdType.MESH
f32 = jnp.float32
bf16 = jnp.bfloat16


def xor4(z, j):
    a, b, c, d = z // 2, z % 2, j // 2, j % 2
    return 2 * (a + c - 2 * a * c) + b + d - 2 * b * d


def fused_kernel(
    tok_ref, grad_ref, g_ref, win_ref, wdown_ref,
    moe_ref, back_ref, nwin_ref, nwdown_ref,
    rows_all, g_all, win, wdown, dproj_all, act_all, dy_all, part, rx, rz,
    gin, gdown, gin_core, gdown_core, gin_y, gdown_y,
    g_send, g_recv, w_send, w_recv, z_send, x_send, row_recv,
    rx_send, rx_recv, rz_send, rz_recv, gc_send, gc_recv, gy_send, gy_recv,
):
    dp = lax.axis_index("dp")
    me = lax.axis_index("expert")
    y, core = dp // 2, dp % 2
    z, x = me // 2, me % 2
    n = tok_ref.shape[0]
    hidden = wdown.shape[0]
    scale_in = win.shape[0] ** -0.5
    scale_down = hidden**-0.5
    q_in, q_down = win_ref.shape[0], wdown_ref.shape[0]
    core_peer = (2 * y + 1 - core, me)
    y_peer = (2 * (1 - y) + core, me)
    x_peer = (dp, 2 * z + 1 - x)
    inner = (z + 1) // 2 % 2

    def copy(src, dst, ssem, rsem, device):
        return pltpu.make_async_remote_copy(
            src_ref=src, dst_ref=dst, send_sem=ssem, recv_sem=rsem,
            device_id=device, device_id_type=MESH,
        )

    def rows(s, size):
        return pl.ds(pl.multiple_of(s * size, 16), size)

    def order(j):
        far = j // 2
        swapped = xor4(z, j + inner * far * (5 - 2 * j))
        return swapped

    rows_all[0, rows(me, n), :] = tok_ref[...]
    rows_all[1, rows(me, n), :] = grad_ref[...]
    g_all[me] = g_ref[...]
    win[rows(dp, q_in), :] = win_ref[...]
    wdown[rows(dp, q_down), :] = wdown_ref[...]

    barrier = pltpu.get_barrier_semaphore()
    for k in range(1, 8):
        pl.semaphore_signal(barrier, inc=1, device_id=(dp, (me + k) % 8), device_id_type=MESH)
    pl.semaphore_signal(barrier, inc=1, device_id=core_peer, device_id_type=MESH)
    pl.semaphore_signal(barrier, inc=1, device_id=y_peer, device_id_type=MESH)
    pl.semaphore_wait(barrier, 9)

    def w_copy(w, k):
        ref, size = ((win, q_in), (wdown, q_down))[w]
        source = 2 * (1 - y) + core if k == 2 else dp
        block = ref.at[rows(source, size), :]
        return copy(block, block, w_send.at[w, k], w_recv.at[w, source], y_peer if k == 0 else core_peer)

    def w_arrive(w, source):
        ref, size = ((win, q_in), (wdown, q_down))[w]
        block = ref.at[rows(source, size), :]
        copy(block, block, w_send.at[w, 0], w_recv.at[w, source], y_peer).wait_recv()

    def g_copy(k):
        return copy(g_all.at[me], g_all.at[me], g_send.at[k - 1], g_recv.at[me], (dp, (me + k) % 8))

    def z_copy(a, j, up):
        s = order(j)
        block = rows_all.at[a, rows(2 * s + x, n), :]
        target = me + 2 if up else me - 2
        return copy(block, block, z_send.at[a, j, up], row_recv.at[a, 2 * s + x], (dp, target))

    def x_copy(a, j):
        s = order(j)
        block = rows_all.at[a, rows(2 * s + x, n), :]
        return copy(block, block, x_send.at[a, j], row_recv.at[a, 2 * s + x], x_peer)

    def row_arrive(a, slot):
        block = rows_all.at[a, rows(slot, n), :]
        copy(block, block, x_send.at[a, 0], row_recv.at[a, slot], x_peer).wait_recv()

    def z_conditions(j):
        s = order(j)
        return (z < 3) & (s <= z), (z > 0) & (s >= z)

    def forward(j):
        go_up, go_down = z_conditions(j)
        for a in range(2):
            if j > 0:
                row_arrive(a, 2 * order(j) + x)

            @pl.when(go_up)
            def _():
                z_copy(a, j, 1).start()

            @pl.when(go_down)
            def _():
                z_copy(a, j, 0).start()

            x_copy(a, j).start()

    for w in range(2):
        w_copy(w, 0).start()
        w_copy(w, 1).start()
    for k in range(1, 8):
        g_copy(k).start()
    forward(0)
    forward(1)
    for w in range(2):
        w_arrive(w, 2 * (1 - y) + core)
        w_copy(w, 2).start()
    forward(2)
    for k in range(1, 8):
        s = (me + k) % 8
        copy(g_all.at[s], g_all.at[s], g_send.at[0], g_recv.at[s], x_peer).wait_recv()
    for w in range(2):
        w_arrive(w, 2 * y + 1 - core)
        w_arrive(w, 2 * (1 - y) + 1 - core)

    nt = (((1,), (1,)), ((), ()))
    tn = (((0,), (0,)), ((), ()))

    def compute(slot):
        at = rows(slot, n)
        by_expert = jnp.transpose(g_all[slot], (1, 0))
        lane = lax.broadcasted_iota(jnp.int32, by_expert.shape, 1)
        g = jnp.sum(jnp.where(lane == me, by_expert, 0.0), axis=1, keepdims=True)
        dy = (g * rows_all[1, at, :].astype(f32)).astype(bf16)
        dy_all[at, :] = dy
        proj = jnp.dot(rows_all[0, at, :], win[...], preferred_element_type=f32) * scale_in
        dact = lax.dot_general(dy, wdown[...], nt, preferred_element_type=f32) * scale_down
        gate, up = proj[:, :hidden], proj[:, hidden:]
        sig = jax.nn.sigmoid(gate)
        silu = gate * sig
        act = (silu * up).astype(bf16)
        act_all[at, :] = act
        dproj_all[at, :hidden] = (dact * up * sig * (1.0 + gate * (1.0 - sig))).astype(bf16)
        dproj_all[at, hidden:] = (dact * silu).astype(bf16)
        out = (jnp.dot(act, wdown[...], preferred_element_type=f32) * scale_down).astype(bf16)
        part[0, at, :] = (g * out.astype(f32)).astype(bf16)
        dx = lax.dot_general(dproj_all[at, :], win[...], nt, preferred_element_type=f32) * scale_in
        part[1, at, :] = dx.astype(bf16)

    def rx_copy(a, s):
        block = part.at[a, rows(2 * s + 1 - x, n), :]
        return copy(block, rx.at[a, s], rx_send.at[a, s], rx_recv.at[a, s], x_peer)

    def step(j, carry):
        @pl.when(j == 1)
        def _():
            forward(3)

        s = order(j)
        compute(2 * s + x)
        row_arrive(0, 2 * s + 1 - x)
        row_arrive(1, 2 * s + 1 - x)
        compute(2 * s + 1 - x)
        return carry

    lax.fori_loop(0, 4, step, 0)
    for j in (3, 2, 1, 0):
        for a in range(2):
            rx_copy(a, order(j)).start()

    for q in range(4):
        gin[q * q_in:(q + 1) * q_in, :] = (
            lax.dot_general(rows_all[0, :, q * q_in:(q + 1) * q_in], dproj_all[...], tn, preferred_element_type=f32) * scale_in
        ).astype(bf16)
    gdown[...] = (lax.dot_general(act_all[...], dy_all[...], tn, preferred_element_type=f32) * scale_down).astype(bf16)

    def gc_copy(w, yy):
        ref, size, dst = ((gin, q_in, gin_core), (gdown, q_down, gdown_core))[w]
        return copy(ref.at[rows(2 * yy + 1 - core, size), :], dst.at[yy], gc_send.at[w, yy], gc_recv.at[w, yy], core_peer)

    def gy_copy(w):
        ref, size, dst = ((gin, q_in, gin_y), (gdown, q_down, gdown_y))[w]
        return copy(ref.at[rows(2 * (1 - y) + core, size), :], dst, gy_send.at[w], gy_recv.at[w], y_peer)

    for w in range(2):
        for yy in range(2):
            gc_copy(w, yy).start()

    def line_copy(a, t, up):
        if up:
            slot, target = t, me + 2
        else:
            slot, target = t + (4 - t) * (1 - jnp.minimum(z - 1 - t, 1)), me - 2
        return copy(part.at[a, rows(2 * t + x, n), :], rz.at[a, slot], rz_send.at[a, t], rz_recv.at[a, slot], (dp, target))

    def line_arrive(a, slot):
        copy(rz.at[a, slot], rz.at[a, slot], rz_send.at[a, 0], rz_recv.at[a, slot], x_peer).wait_recv()

    def line(t):
        for a in range(2):
            at = rows(2 * t + x, n)

            @pl.when(z != t)
            def _():
                rx_copy(a, t).wait_recv()

                @pl.when(((z < t) & (z > 0)) | ((z > t) & (z < 3)))
                def _():
                    line_arrive(a, t)
                    part[a, at, :] = (
                        part[a, at, :].astype(f32) + rx[a, t].astype(f32) + rz[a, t].astype(f32)
                    ).astype(bf16)

                @pl.when(((z < t) & (z == 0)) | ((z > t) & (z == 3)))
                def _():
                    part[a, at, :] = (part[a, at, :].astype(f32) + rx[a, t].astype(f32)).astype(bf16)

            @pl.when(z < t)
            def _():
                line_copy(a, t, 1).start()

            @pl.when(z > t)
            def _():
                line_copy(a, t, 0).start()

    line(3)
    line(0)
    for w in range(2):
        ref, size, got = ((gin, q_in, gin_core), (gdown, q_down, gdown_core))[w]
        gc_copy(w, 0).wait_recv()
        gc_copy(w, 1).wait_recv()
        at = rows(2 * (1 - y) + core, size)
        ref[at, :] = (ref[at, :].astype(f32) + got[1 - y].astype(f32)).astype(bf16)
        gy_copy(w).start()
    line(2)
    line(1)

    for w in range(2):
        ref, size, got, far, old, new = (
            (gin, q_in, gin_core, gin_y, win_ref, nwin_ref),
            (gdown, q_down, gdown_core, gdown_y, wdown_ref, nwdown_ref),
        )[w]
        gy_copy(w).wait_recv()
        total = ref[rows(dp, size), :].astype(f32) + got[y].astype(f32) + far[...].astype(f32)
        new[...] = (old[...].astype(f32) - step_rate * total).astype(bf16)

    for a in range(2):
        out = (moe_ref, back_ref)[a]
        rx_copy(a, z).wait_recv()
        own = part[a, rows(me, n), :].astype(f32) + rx[a, z].astype(f32)

        @pl.when(z == 0)
        def _():
            line_arrive(a, 4)
            out[...] = (own + rz[a, 4].astype(f32)).astype(bf16)

        @pl.when(z == 3)
        def _():
            line_arrive(a, 3)
            out[...] = (own + rz[a, 3].astype(f32)).astype(bf16)

        @pl.when((z > 0) & (z < 3))
        def _():
            line_arrive(a, z)
            line_arrive(a, 4)
            out[...] = (own + rz[a, z].astype(f32) + rz[a, 4].astype(f32)).astype(bf16)

    for w in range(2):
        for k in range(3):
            w_copy(w, k).wait_send()
        for yy in range(2):
            gc_copy(w, yy).wait_send()
        gy_copy(w).wait_send()
    for k in range(1, 8):
        g_copy(k).wait_send()
    for a in range(2):
        for j in range(4):
            go_up, go_down = z_conditions(j)

            @pl.when(go_up)
            def _():
                z_copy(a, j, 1).wait_send()

            @pl.when(go_down)
            def _():
                z_copy(a, j, 0).wait_send()

            x_copy(a, j).wait_send()
            rx_copy(a, j).wait_send()

            @pl.when(z < j)
            def _():
                line_copy(a, j, 1).wait_send()

            @pl.when(z > j)
            def _():
                line_copy(a, j, 0).wait_send()


def fused_body(tokens, routes, gates, w_in, w_down, out_grad):
    n, width = tokens.shape
    hidden = w_in.shape[2] // 2
    q_in, q_down = w_in.shape[1], w_down.shape[1]
    hit = routes.T[:, None, :] == jnp.arange(8, dtype=jnp.int32)[None, :, None]
    weight = jnp.sum(jnp.where(hit, gates.T[:, None, :], 0.0), axis=0)
    vmem = pl.BlockSpec(memory_space=pltpu.VMEM)
    dma = pltpu.SemaphoreType.DMA
    buf = pltpu.VMEM
    outs = pl.pallas_call(
        fused_kernel,
        out_shape=(
            jax.ShapeDtypeStruct((n, width), bf16),
            jax.ShapeDtypeStruct((n, width), bf16),
            jax.ShapeDtypeStruct((q_in, 2 * hidden), bf16),
            jax.ShapeDtypeStruct((q_down, width), bf16),
        ),
        in_specs=[vmem] * 5,
        out_specs=(vmem,) * 4,
        scratch_shapes=[
            buf((2, 8 * n, width), bf16),
            buf((8, 8, n), f32),
            buf((4 * q_in, 2 * hidden), bf16),
            buf((4 * q_down, width), bf16),
            buf((8 * n, 2 * hidden), bf16),
            buf((8 * n, hidden), bf16),
            buf((8 * n, width), bf16),
            buf((2, 8 * n, width), bf16),
            buf((2, 4, n, width), bf16),
            buf((2, 5, n, width), bf16),
            buf((4 * q_in, 2 * hidden), bf16),
            buf((4 * q_down, width), bf16),
            buf((2, q_in, 2 * hidden), bf16),
            buf((2, q_down, width), bf16),
            buf((q_in, 2 * hidden), bf16),
            buf((q_down, width), bf16),
            dma((7,)), dma((8,)), dma((2, 3)), dma((2, 4)), dma((2, 4, 2)), dma((2, 4)), dma((2, 8)),
            dma((2, 4)), dma((2, 4)), dma((2, 4)), dma((2, 5)), dma((2, 2)), dma((2, 2)), dma((2,)), dma((2,)),
        ],
        compiler_params=pltpu.CompilerParams(
            collective_id=0, has_side_effects=True, vmem_limit_bytes=48 * 1024 * 1024
        ),
    )(tokens, out_grad, weight, w_in[0], w_down[0])
    return (outs[0], outs[1], outs[2][None], outs[3][None])


def solution(mesh):
    fused = mesh.shape["dp"] == 4 and mesh.shape["expert"] == 8
    return jax.shard_map(
        fused_body if fused else body,
        mesh=mesh,
        in_specs=(
            P(("dp", "expert"), None),
            P(("dp", "expert"), None),
            P(("dp", "expert"), None),
            P("expert", "dp", None),
            P("expert", "dp", None),
            P(("dp", "expert"), None),
        ),
        out_specs=(
            P(("dp", "expert"), None),
            P(("dp", "expert"), None),
            P("expert", "dp", None),
            P("expert", "dp", None),
        ),
        check_vma=False,
    )
```

```python
import jax
import jax.numpy as jnp
from jax import lax
from jax.experimental import pallas as pl
from jax.experimental.pallas import tpu as pltpu
from jax.sharding import PartitionSpec as P

step_rate = 0.5


def expert_gates(routes, gates, experts):
    hit = routes[:, :, None] == jnp.arange(experts, dtype=jnp.int32)[None, None, :]
    return jnp.sum(jnp.where(hit, gates[:, :, None], 0.0), axis=1)


def body(tokens, routes, gates, w_in, w_down, out_grad):
    model_width = tokens.shape[1]
    hidden = w_in.shape[2] // 2
    per_device = w_in.shape[0]
    experts = per_device * lax.axis_size("expert")
    scale_in = model_width**-0.5
    scale_down = hidden**-0.5
    f32 = jnp.float32
    full_in = lax.all_gather(w_in, "dp", axis=1, tiled=True)
    all_tokens = lax.all_gather(tokens, "expert", axis=0, tiled=True)
    all_grads = lax.all_gather(out_grad, "expert", axis=0, tiled=True)
    full_down = lax.all_gather(w_down, "dp", axis=1, tiled=True)
    weight = lax.all_gather(expert_gates(routes, gates, experts), "expert", axis=0, tiled=True)
    first = lax.axis_index("expert") * per_device
    moe, back, grads_in, grads_down = 0.0, 0.0, [], []
    for local in range(per_device):
        win, wdown = full_in[local], full_down[local]
        g = lax.dynamic_slice_in_dim(weight, first + local, 1, axis=1)
        proj = jnp.dot(all_tokens, win, preferred_element_type=f32) * scale_in
        gate, up = proj[:, :hidden], proj[:, hidden:]
        sig = jax.nn.sigmoid(gate)
        act = (gate * sig * up).astype(jnp.bfloat16)
        y = (jnp.dot(act, wdown, preferred_element_type=f32) * scale_down).astype(jnp.bfloat16)
        moe = moe + g * y.astype(f32)
        dy = (g * all_grads.astype(f32)).astype(jnp.bfloat16)
        dact = lax.dot_general(dy, wdown, (((1,), (1,)), ((), ())), preferred_element_type=f32) * scale_down
        dproj = jnp.concatenate(
            [dact * up * sig * (1.0 + gate * (1.0 - sig)), dact * gate * sig], axis=-1
        ).astype(jnp.bfloat16)
        dx = lax.dot_general(dproj, win, (((1,), (1,)), ((), ())), preferred_element_type=f32) * scale_in
        back = back + dx.astype(jnp.bfloat16).astype(f32)
        grads_in.append(
            (lax.dot_general(all_tokens, dproj, (((0,), (0,)), ((), ())), preferred_element_type=f32) * scale_in).astype(jnp.bfloat16)
        )
        grads_down.append(
            (lax.dot_general(act, dy, (((0,), (0,)), ((), ())), preferred_element_type=f32) * scale_down).astype(jnp.bfloat16)
        )
    moe_out = lax.psum_scatter(moe.astype(jnp.bfloat16), "expert", scatter_dimension=0, tiled=True)
    token_grad = lax.psum_scatter(back.astype(jnp.bfloat16), "expert", scatter_dimension=0, tiled=True)
    sum_in = lax.psum_scatter(jnp.stack(grads_in), "dp", scatter_dimension=1, tiled=True)
    sum_down = lax.psum_scatter(jnp.stack(grads_down), "dp", scatter_dimension=1, tiled=True)
    new_w_in = (w_in.astype(f32) - step_rate * sum_in.astype(f32)).astype(jnp.bfloat16)
    new_w_down = (w_down.astype(f32) - step_rate * sum_down.astype(f32)).astype(jnp.bfloat16)
    return (moe_out, token_grad, new_w_in, new_w_down)


MESH = pl.DeviceIdType.MESH
f32 = jnp.float32
bf16 = jnp.bfloat16


def xor4(z, j):
    a, b, c, d = z // 2, z % 2, j // 2, j % 2
    return 2 * (a + c - 2 * a * c) + b + d - 2 * b * d


def fused_kernel(
    tok_ref, grad_ref, g_ref, win_ref, wdown_ref,
    moe_ref, back_ref, nwin_ref, nwdown_ref,
    rows_all, g_all, win, wdown, dproj_all, act_all, dy_all, part, rx, rz,
    gin, gdown, gin_core, gdown_core, gin_y, gdown_y,
    g_send, g_recv, w_send, w_recv, z_send, x_send, row_recv,
    rx_send, rx_recv, rz_send, rz_recv, gc_send, gc_recv, gy_send, gy_recv,
):
    dp = lax.axis_index("dp")
    me = lax.axis_index("expert")
    y, core = dp // 2, dp % 2
    z, x = me // 2, me % 2
    n = tok_ref.shape[0]
    hidden = wdown.shape[0]
    scale_in = win.shape[0] ** -0.5
    scale_down = hidden**-0.5
    q_in, q_down = win_ref.shape[0], wdown_ref.shape[0]
    core_peer = (2 * y + 1 - core, me)
    y_peer = (2 * (1 - y) + core, me)
    x_peer = (dp, 2 * z + 1 - x)
    inner = (z + 1) // 2 % 2

    def copy(src, dst, ssem, rsem, device):
        return pltpu.make_async_remote_copy(
            src_ref=src, dst_ref=dst, send_sem=ssem, recv_sem=rsem,
            device_id=device, device_id_type=MESH,
        )

    def rows(s, size):
        return pl.ds(pl.multiple_of(s * size, 16), size)

    def order(j):
        far = j // 2
        swapped = xor4(z, j + inner * far * (5 - 2 * j))
        return swapped

    rows_all[0, rows(me, n), :] = tok_ref[...]
    rows_all[1, rows(me, n), :] = grad_ref[...]
    g_all[me] = g_ref[...]
    win[rows(dp, q_in), :] = win_ref[...]
    wdown[rows(dp, q_down), :] = wdown_ref[...]

    barrier = pltpu.get_barrier_semaphore()
    for k in range(1, 8):
        pl.semaphore_signal(barrier, inc=1, device_id=(dp, (me + k) % 8), device_id_type=MESH)
    pl.semaphore_signal(barrier, inc=1, device_id=core_peer, device_id_type=MESH)
    pl.semaphore_signal(barrier, inc=1, device_id=y_peer, device_id_type=MESH)
    pl.semaphore_wait(barrier, 9)

    def w_copy(w, k):
        ref, size = ((win, q_in), (wdown, q_down))[w]
        source = 2 * (1 - y) + core if k == 2 else dp
        block = ref.at[rows(source, size), :]
        return copy(block, block, w_send.at[w, k], w_recv.at[w, source], y_peer if k == 0 else core_peer)

    def w_arrive(w, source):
        ref, size = ((win, q_in), (wdown, q_down))[w]
        block = ref.at[rows(source, size), :]
        copy(block, block, w_send.at[w, 0], w_recv.at[w, source], y_peer).wait_recv()

    def g_copy(k):
        return copy(g_all.at[me], g_all.at[me], g_send.at[k - 1], g_recv.at[me], (dp, (me + k) % 8))

    def z_copy(a, j, up):
        s = order(j)
        block = rows_all.at[a, rows(2 * s + x, n), :]
        target = me + 2 if up else me - 2
        return copy(block, block, z_send.at[a, j, up], row_recv.at[a, 2 * s + x], (dp, target))

    def x_copy(a, j):
        s = order(j)
        block = rows_all.at[a, rows(2 * s + x, n), :]
        return copy(block, block, x_send.at[a, j], row_recv.at[a, 2 * s + x], x_peer)

    def row_arrive(a, slot):
        block = rows_all.at[a, rows(slot, n), :]
        copy(block, block, x_send.at[a, 0], row_recv.at[a, slot], x_peer).wait_recv()

    def z_conditions(j):
        s = order(j)
        return (z < 3) & (s <= z), (z > 0) & (s >= z)

    def forward(j):
        go_up, go_down = z_conditions(j)
        for a in range(2):
            if j > 0:
                row_arrive(a, 2 * order(j) + x)

            @pl.when(go_up)
            def _():
                z_copy(a, j, 1).start()

            @pl.when(go_down)
            def _():
                z_copy(a, j, 0).start()

            x_copy(a, j).start()

    for w in range(2):
        w_copy(w, 0).start()
        w_copy(w, 1).start()
    for k in range(1, 8):
        g_copy(k).start()
    forward(0)
    forward(1)
    for w in range(2):
        w_arrive(w, 2 * (1 - y) + core)
        w_copy(w, 2).start()
    forward(2)
    for k in range(1, 8):
        s = (me + k) % 8
        copy(g_all.at[s], g_all.at[s], g_send.at[0], g_recv.at[s], x_peer).wait_recv()
    for w in range(2):
        w_arrive(w, 2 * y + 1 - core)
        w_arrive(w, 2 * (1 - y) + 1 - core)

    nt = (((1,), (1,)), ((), ()))
    tn = (((0,), (0,)), ((), ()))

    def compute(slot):
        at = rows(slot, n)
        by_expert = jnp.transpose(g_all[slot], (1, 0))
        lane = lax.broadcasted_iota(jnp.int32, by_expert.shape, 1)
        g = jnp.sum(jnp.where(lane == me, by_expert, 0.0), axis=1, keepdims=True)
        dy = (g * rows_all[1, at, :].astype(f32)).astype(bf16)
        dy_all[at, :] = dy
        proj = jnp.dot(rows_all[0, at, :], win[...], preferred_element_type=f32) * scale_in
        dact = lax.dot_general(dy, wdown[...], nt, preferred_element_type=f32) * scale_down
        gate, up = proj[:, :hidden], proj[:, hidden:]
        sig = jax.nn.sigmoid(gate)
        silu = gate * sig
        act = (silu * up).astype(bf16)
        act_all[at, :] = act
        dproj_all[at, :hidden] = (dact * up * sig * (1.0 + gate * (1.0 - sig))).astype(bf16)
        dproj_all[at, hidden:] = (dact * silu).astype(bf16)
        out = (jnp.dot(act, wdown[...], preferred_element_type=f32) * scale_down).astype(bf16)
        part[0, at, :] = (g * out.astype(f32)).astype(bf16)
        dx = lax.dot_general(dproj_all[at, :], win[...], nt, preferred_element_type=f32) * scale_in
        part[1, at, :] = dx.astype(bf16)

    def rx_copy(a, s):
        block = part.at[a, rows(2 * s + 1 - x, n), :]
        return copy(block, rx.at[a, s], rx_send.at[a, s], rx_recv.at[a, s], x_peer)

    def step(j, carry):
        @pl.when(j == 1)
        def _():
            forward(3)

        s = order(j)
        compute(2 * s + x)
        row_arrive(0, 2 * s + 1 - x)
        row_arrive(1, 2 * s + 1 - x)
        compute(2 * s + 1 - x)
        return carry

    lax.fori_loop(0, 4, step, 0)
    for a in range(2):
        for j in (3, 2, 1, 0):
            rx_copy(a, order(j)).start()

    for q in range(4):
        gin[q * q_in:(q + 1) * q_in, :] = (
            lax.dot_general(rows_all[0, :, q * q_in:(q + 1) * q_in], dproj_all[...], tn, preferred_element_type=f32) * scale_in
        ).astype(bf16)
    gdown[...] = (lax.dot_general(act_all[...], dy_all[...], tn, preferred_element_type=f32) * scale_down).astype(bf16)

    def gc_copy(w, yy):
        ref, size, dst = ((gin, q_in, gin_core), (gdown, q_down, gdown_core))[w]
        return copy(ref.at[rows(2 * yy + 1 - core, size), :], dst.at[yy], gc_send.at[w, yy], gc_recv.at[w, yy], core_peer)

    def gy_copy(w):
        ref, size, dst = ((gin, q_in, gin_y), (gdown, q_down, gdown_y))[w]
        return copy(ref.at[rows(2 * (1 - y) + core, size), :], dst, gy_send.at[w], gy_recv.at[w], y_peer)

    for w in range(2):
        for yy in range(2):
            gc_copy(w, yy).start()

    def line_copy(a, t, up):
        if up:
            slot, target = t, me + 2
        else:
            slot, target = t + (4 - t) * (1 - jnp.minimum(z - 1 - t, 1)), me - 2
        return copy(part.at[a, rows(2 * t + x, n), :], rz.at[a, slot], rz_send.at[a, t], rz_recv.at[a, slot], (dp, target))

    def line_arrive(a, slot):
        copy(rz.at[a, slot], rz.at[a, slot], rz_send.at[a, 0], rz_recv.at[a, slot], x_peer).wait_recv()

    def line(a, t):
        if True:
            at = rows(2 * t + x, n)

            @pl.when(z != t)
            def _():
                rx_copy(a, t).wait_recv()

                @pl.when(((z < t) & (z > 0)) | ((z > t) & (z < 3)))
                def _():
                    line_arrive(a, t)
                    part[a, at, :] = (
                        part[a, at, :].astype(f32) + rx[a, t].astype(f32) + rz[a, t].astype(f32)
                    ).astype(bf16)

                @pl.when(((z < t) & (z == 0)) | ((z > t) & (z == 3)))
                def _():
                    part[a, at, :] = (part[a, at, :].astype(f32) + rx[a, t].astype(f32)).astype(bf16)

            @pl.when(z < t)
            def _():
                line_copy(a, t, 1).start()

            @pl.when(z > t)
            def _():
                line_copy(a, t, 0).start()

    for w in range(2):
        ref, size, got = ((gin, q_in, gin_core), (gdown, q_down, gdown_core))[w]
        gc_copy(w, 0).wait_recv()
        gc_copy(w, 1).wait_recv()
        at = rows(2 * (1 - y) + core, size)
        ref[at, :] = (ref[at, :].astype(f32) + got[1 - y].astype(f32)).astype(bf16)
        gy_copy(w).start()
    for a in range(2):
        for t in (3, 0, 2, 1):
            line(a, t)

    for w in range(2):
        ref, size, got, far, old, new = (
            (gin, q_in, gin_core, gin_y, win_ref, nwin_ref),
            (gdown, q_down, gdown_core, gdown_y, wdown_ref, nwdown_ref),
        )[w]
        gy_copy(w).wait_recv()
        total = ref[rows(dp, size), :].astype(f32) + got[y].astype(f32) + far[...].astype(f32)
        new[...] = (old[...].astype(f32) - step_rate * total).astype(bf16)

    for a in range(2):
        out = (moe_ref, back_ref)[a]
        rx_copy(a, z).wait_recv()
        own = part[a, rows(me, n), :].astype(f32) + rx[a, z].astype(f32)

        @pl.when(z == 0)
        def _():
            line_arrive(a, 4)
            out[...] = (own + rz[a, 4].astype(f32)).astype(bf16)

        @pl.when(z == 3)
        def _():
            line_arrive(a, 3)
            out[...] = (own + rz[a, 3].astype(f32)).astype(bf16)

        @pl.when((z > 0) & (z < 3))
        def _():
            line_arrive(a, z)
            line_arrive(a, 4)
            out[...] = (own + rz[a, z].astype(f32) + rz[a, 4].astype(f32)).astype(bf16)

    for w in range(2):
        for k in range(3):
            w_copy(w, k).wait_send()
        for yy in range(2):
            gc_copy(w, yy).wait_send()
        gy_copy(w).wait_send()
    for k in range(1, 8):
        g_copy(k).wait_send()
    for a in range(2):
        for j in range(4):
            go_up, go_down = z_conditions(j)

            @pl.when(go_up)
            def _():
                z_copy(a, j, 1).wait_send()

            @pl.when(go_down)
            def _():
                z_copy(a, j, 0).wait_send()

            x_copy(a, j).wait_send()
            rx_copy(a, j).wait_send()

            @pl.when(z < j)
            def _():
                line_copy(a, j, 1).wait_send()

            @pl.when(z > j)
            def _():
                line_copy(a, j, 0).wait_send()


def fused_body(tokens, routes, gates, w_in, w_down, out_grad):
    n, width = tokens.shape
    hidden = w_in.shape[2] // 2
    q_in, q_down = w_in.shape[1], w_down.shape[1]
    hit = routes.T[:, None, :] == jnp.arange(8, dtype=jnp.int32)[None, :, None]
    weight = jnp.sum(jnp.where(hit, gates.T[:, None, :], 0.0), axis=0)
    vmem = pl.BlockSpec(memory_space=pltpu.VMEM)
    dma = pltpu.SemaphoreType.DMA
    buf = pltpu.VMEM
    outs = pl.pallas_call(
        fused_kernel,
        out_shape=(
            jax.ShapeDtypeStruct((n, width), bf16),
            jax.ShapeDtypeStruct((n, width), bf16),
            jax.ShapeDtypeStruct((q_in, 2 * hidden), bf16),
            jax.ShapeDtypeStruct((q_down, width), bf16),
        ),
        in_specs=[vmem] * 5,
        out_specs=(vmem,) * 4,
        scratch_shapes=[
            buf((2, 8 * n, width), bf16),
            buf((8, 8, n), f32),
            buf((4 * q_in, 2 * hidden), bf16),
            buf((4 * q_down, width), bf16),
            buf((8 * n, 2 * hidden), bf16),
            buf((8 * n, hidden), bf16),
            buf((8 * n, width), bf16),
            buf((2, 8 * n, width), bf16),
            buf((2, 4, n, width), bf16),
            buf((2, 5, n, width), bf16),
            buf((4 * q_in, 2 * hidden), bf16),
            buf((4 * q_down, width), bf16),
            buf((2, q_in, 2 * hidden), bf16),
            buf((2, q_down, width), bf16),
            buf((q_in, 2 * hidden), bf16),
            buf((q_down, width), bf16),
            dma((7,)), dma((8,)), dma((2, 3)), dma((2, 4)), dma((2, 4, 2)), dma((2, 4)), dma((2, 8)),
            dma((2, 4)), dma((2, 4)), dma((2, 4)), dma((2, 5)), dma((2, 2)), dma((2, 2)), dma((2,)), dma((2,)),
        ],
        compiler_params=pltpu.CompilerParams(
            collective_id=0, has_side_effects=True, vmem_limit_bytes=48 * 1024 * 1024
        ),
    )(tokens, out_grad, weight, w_in[0], w_down[0])
    return (outs[0], outs[1], outs[2][None], outs[3][None])


def solution(mesh):
    fused = mesh.shape["dp"] == 4 and mesh.shape["expert"] == 8
    return jax.shard_map(
        fused_body if fused else body,
        mesh=mesh,
        in_specs=(
            P(("dp", "expert"), None),
            P(("dp", "expert"), None),
            P(("dp", "expert"), None),
            P("expert", "dp", None),
            P("expert", "dp", None),
            P(("dp", "expert"), None),
        ),
        out_specs=(
            P(("dp", "expert"), None),
            P(("dp", "expert"), None),
            P("expert", "dp", None),
            P("expert", "dp", None),
        ),
        check_vma=False,
    )
```
